32 devices in a mesh: doc: 2 (over y), seq: 4 (over z), sub: 4 (over x, core).
Axes of the slice: x: 2, y: 2, z: 4, core: 2. Of those that a mesh axis runs over, the one named last changes fastest.
Arguments:
- queries: bfloat16 [16384, 512], P(('doc', 'seq', 'sub')), parts along dimension 0, may hold values from -18 to 18
- keys: bfloat16 [16384, 512], P(('doc', 'seq', 'sub')), parts along dimension 0, may hold values from -18 to 18
- values: bfloat16 [16384, 512], P(('doc', 'seq', 'sub')), parts along dimension 0, may hold values from -18 to 18
- seg_lengths: int32 [512], P('doc'), parts along dimension 0, may hold values from 1 to 64, 8192 in all
Outputs:
- attended: bfloat16 [16384, 512], P(('doc', 'seq', 'sub')), parts along dimension 0
The draws below stay inside these ranges and needn't reach their ends.
There are 2 independent parts, one for each index of `doc`. The reference program is written for one: setup_inputs(seed, part) draws one part's arguments, and reference() takes and returns one part's arrays. A program takes and returns all parts, laid end to end along the dimension named above; each array names one. Nothing has to cross between parts.
Inputs may be any that keep to these rules, and one draw needn't show every extreme that they name: `seg_lengths`: the 256 segments cover all 8192 tokens in order; the longest has exactly 64 tokens.
All inputs are finite; a program needn't handle non-finite values.
Results may differ from the reference program's by a relative error of at most 0.012.
Values may be sent and summed in bfloat16 or wider, within the bound.
A program may use at most 64 MiB of HBM per device.

```python
import math
import jax
import jax.numpy as jnp
import numpy as np
from jax import lax

H = 8
HD = 64
M = 256
ITERS = 3
TOK_DEV = 512
TOKENS = 8192
MOST = 64


def token_field(key, salt):
    width = H * HD
    base = jax.random.fold_in(key, salt)
    noise_key, region_key = jax.random.split(base, 2)
    region = jnp.clip(jax.random.normal(region_key, (M, width), jnp.float32), -4.0, 4.0) * 1.5
    spread = jnp.repeat(region, TOKENS // M, axis=0)
    noise = jnp.clip(jax.random.normal(noise_key, (TOKENS, width), jnp.float32), -5.0, 5.0)
    field = noise + spread
    return field


def draw_queries(key, part):
    return token_field(key, 11).astype(jnp.bfloat16)


def draw_keys(key, part):
    return token_field(key, 23).astype(jnp.bfloat16)


def draw_values(key, part):
    return token_field(key, 37).astype(jnp.bfloat16)


def length_profile(count, total, bound, skew):
    weights = [(1 << 20) // math.isqrt(rank ** skew) + 1 for rank in range(2, count + 1)]
    spare, holding = total - bound - (count - 1), [1] * (count - 1)
    while spare > 0:
        movable = [i for i in range(count - 1) if holding[i] < bound]
        mass, left = sum([weights[i] for i in movable]), spare
        for i in movable:
            addition = min(bound - holding[i], max(1, left * weights[i] // mass), spare)
            holding[i] = holding[i] + addition
            spare = spare - addition
    return np.array([bound] + holding)


def ragged(stream_key, count, total, reach, skew):
    if count == 2:
        one = jax.random.randint(stream_key, (), max(1, total - reach), min(reach, total - 1) + 1)
        return jnp.stack([one, total - one])
    tallies = jnp.asarray(length_profile(count, total, reach, skew), jnp.int32)
    twos = (count - 1) // 2
    donor, receiver = tallies[1:1 + 2 * twos:2], tallies[2:2 + 2 * twos:2]
    slack = jnp.minimum(donor - 1, reach - receiver)
    shifted = jax.random.randint(jax.random.fold_in(stream_key, 1), (twos,), 0, 1 << 20) % (slack + 1)
    tallies = tallies.at[1:1 + 2 * twos:2].set(donor - shifted).at[2:2 + 2 * twos:2].set(receiver + shifted)
    return tallies[jax.random.permutation(jax.random.fold_in(stream_key, 2), count)]


def setup_inputs(seed: int = 0, part: int = 0) -> dict:
    splits = jax.random.split(jax.random.key(seed), 5)
    own_keys = jax.random.split(jax.random.fold_in(splits[4], part), 5)
    return {
        "queries": draw_queries(jax.random.fold_in(jax.random.fold_in(splits[4], part), 71), part),
        "keys": draw_keys(jax.random.fold_in(jax.random.fold_in(splits[4], part), 71), part),
        "values": draw_values(jax.random.fold_in(jax.random.fold_in(splits[4], part), 71), part),
        "seg_lengths": ragged(own_keys[3], M, TOKENS, MOST, 1).astype(jnp.int32),
    }


HIGH_PRECISION = lax.Precision.HIGHEST

def row_softmax(score_matrix):
    row_top = lax.optimization_barrier(jnp.max(score_matrix, axis=-1, keepdims=True))
    exponentials = jnp.exp(score_matrix - row_top)
    return exponentials / lax.optimization_barrier(jnp.sum(exponentials, axis=-1, keepdims=True))

def iterative_pseudo_inverse(kernel):
    absval = jnp.abs(kernel)
    row_most = lax.optimization_barrier(jnp.max(lax.optimization_barrier(jnp.sum(absval, axis=2)), axis=1))
    col_most = lax.optimization_barrier(jnp.max(lax.optimization_barrier(jnp.sum(absval, axis=1)), axis=1))
    iterate = jnp.transpose(kernel, (0, 2, 1)) / (row_most * col_most)[:, None, None]
    identity = jnp.eye(kernel.shape[1], dtype=jnp.float32)[None]
    for sweep in range(ITERS):
        product = jnp.einsum('hij,hjk->hik', kernel, iterate, precision=HIGH_PRECISION)
        nested = jnp.einsum('hij,hjk->hik', product, 7.0 * identity - product, precision=HIGH_PRECISION)
        nested = jnp.einsum('hij,hjk->hik', product, 15.0 * identity - nested, precision=HIGH_PRECISION)
        iterate = 0.25 * jnp.einsum('hij,hjk->hik', iterate, 13.0 * identity - nested, precision=HIGH_PRECISION)
    return iterate

def reference(queries, keys, values, seg_lengths):
    score_scaling = 1.0 / math.sqrt(HD)
    positions = jnp.arange(TOKENS, dtype=jnp.int32)
    seg_ends = jnp.cumsum(seg_lengths).astype(jnp.int32)
    segment = jnp.searchsorted(seg_ends, positions, side='right').astype(jnp.int32)
    counts = seg_lengths.astype(jnp.float32)
    q_sums = jax.ops.segment_sum(queries.astype(jnp.float32), segment, num_segments=M)
    k_sums = jax.ops.segment_sum(keys.astype(jnp.float32), segment, num_segments=M)
    query_landmarks = (q_sums / counts[:, None]).astype(jnp.bfloat16).reshape(M, H, HD)
    key_landmarks = (k_sums / counts[:, None]).astype(jnp.bfloat16).reshape(M, H, HD)
    landmark_kernel = row_softmax(jnp.einsum('raj,taj->art', query_landmarks.astype(jnp.float32), key_landmarks.astype(jnp.float32)) * score_scaling)
    keys_heads = keys.reshape(TOKENS, H, HD).transpose(1, 0, 2)
    vals_heads = values.reshape(TOKENS, H, HD).transpose(1, 0, 2)

    def one_head(items):
        land_head, key_head, val_head = items
        score_matrix = jnp.dot(land_head, key_head.T, preferred_element_type=jnp.float32) * score_scaling
        row_top = lax.optimization_barrier(jnp.max(score_matrix, axis=1, keepdims=True))
        exponentials = jnp.exp(score_matrix - row_top)
        total = lax.optimization_barrier(jnp.sum(exponentials, axis=1))
        numer = jnp.dot(exponentials, val_head.astype(jnp.float32), precision=HIGH_PRECISION)
        return numer / total[:, None]
    landmark_values = lax.map(one_head, (query_landmarks.transpose(1, 0, 2), keys_heads, vals_heads))
    mixing_matrix = jnp.einsum('gux,gxr->gur', iterative_pseudo_inverse(landmark_kernel), landmark_values, precision=HIGH_PRECISION).astype(jnp.bfloat16)
    q_blocks = queries.reshape(TOKENS // TOK_DEV, TOK_DEV, H, HD)

    def one_block(block_matrix):
        score_matrix = jnp.einsum('fxp,oxp->fxo', block_matrix.astype(jnp.float32), key_landmarks.astype(jnp.float32)) * score_scaling
        weight_matrix = row_softmax(score_matrix).astype(jnp.bfloat16)
        mixed_output = jnp.einsum('ugf,gfa->uga', weight_matrix.astype(jnp.float32), mixing_matrix.astype(jnp.float32))
        return mixed_output.reshape(TOK_DEV, H * HD).astype(jnp.bfloat16)
    return lax.map(one_block, q_blocks).reshape(TOKENS, H * HD)
```

```python
import functools
import math

import jax
import jax.numpy as jnp
from jax import lax
from jax.experimental import pallas as pl
from jax.experimental.pallas import tpu as pltpu
from jax.sharding import PartitionSpec as P

H = 8
HD = 64
M = 256
ITERS = 3


HIGH_PRECISION = lax.Precision.HIGHEST


def row_softmax(score_matrix):
    row_top = lax.optimization_barrier(jnp.max(score_matrix, axis=-1, keepdims=True))
    exponentials = jnp.exp(score_matrix - row_top)
    return exponentials / lax.optimization_barrier(jnp.sum(exponentials, axis=-1, keepdims=True))


def iterative_pseudo_inverse(kernel):
    absval = jnp.abs(kernel)
    row_most = jnp.max(jnp.sum(absval, axis=2), axis=1)
    col_most = jnp.max(jnp.sum(absval, axis=1), axis=1)
    iterate = jnp.transpose(kernel, (0, 2, 1)) / (row_most * col_most)[:, None, None]
    identity = jnp.eye(kernel.shape[1], dtype=jnp.float32)[None]
    for sweep in range(ITERS):
        product = jnp.einsum("hij,hjk->hik", kernel, iterate, precision=HIGH_PRECISION)
        nested = jnp.einsum(
            "hij,hjk->hik", product, 7.0 * identity - product, precision=HIGH_PRECISION
        )
        nested = jnp.einsum(
            "hij,hjk->hik", product, 15.0 * identity - nested, precision=HIGH_PRECISION
        )
        iterate = 0.25 * jnp.einsum(
            "hij,hjk->hik", iterate, 13.0 * identity - nested, precision=HIGH_PRECISION
        )
    return iterate


def solve_mixing(query_head_rows, key_head_rows, landmark_values, score_scaling):
    landmark_kernel = row_softmax(
        jnp.einsum(
            "raj,taj->art", query_head_rows, key_head_rows, preferred_element_type=jnp.float32
        )
        * score_scaling
    )
    approx_inverse = iterative_pseudo_inverse(landmark_kernel)
    return jnp.einsum(
        "gux,gxr->gur", approx_inverse, landmark_values, precision=HIGH_PRECISION
    ).astype(jnp.bfloat16)


def shards(queries, keys, values, seg_lengths):
    row_count = queries.shape[0]
    width = queries.shape[1]
    score_scaling = 1.0 / math.sqrt(HD)
    shard = lax.axis_index("seq") * lax.axis_size("sub") + lax.axis_index("sub")
    positions = shard * row_count + lax.iota(jnp.int32, row_count)
    earlier = lax.broadcasted_iota(jnp.int32, (M, M), 0) <= lax.broadcasted_iota(jnp.int32, (M, M), 1)
    seg_ends = jnp.sum(jnp.where(earlier, seg_lengths[:, None], 0), axis=0)
    seg_begins = seg_ends - seg_lengths
    member = (
        (positions[:, None] >= seg_begins[None, :]) & (positions[:, None] < seg_ends[None, :])
    ).astype(jnp.bfloat16)
    counts = seg_lengths.astype(jnp.float32)
    contract = (((0,), (0,)), ((), ()))
    q_part = lax.dot_general(member, queries, contract, preferred_element_type=jnp.float32)
    k_part = lax.dot_general(member, keys, contract, preferred_element_type=jnp.float32)
    q_sums, k_sums = lax.psum((q_part, k_part), ("seq", "sub"))
    query_landmarks = (q_sums / counts[:, None]).astype(jnp.bfloat16)
    key_landmarks = (k_sums / counts[:, None]).astype(jnp.bfloat16)
    query_head_rows = query_landmarks.reshape(M, H, HD)
    key_head_rows = key_landmarks.reshape(M, H, HD)
    value_head_rows = values.reshape(row_count, H, HD)
    score_matrix = (
        jnp.einsum(
            "czy,rzy->zcr",
            query_head_rows,
            keys.reshape(row_count, H, HD),
            preferred_element_type=jnp.float32,
        )
        * score_scaling
    )
    row_top = lax.pmax(jnp.max(score_matrix, axis=2), ("seq", "sub"))
    exponentials = jnp.exp(score_matrix - row_top[:, :, None])
    total = jnp.sum(exponentials, axis=2)
    numer = jnp.einsum(
        "ijv,vib->ijb",
        exponentials,
        value_head_rows,
        precision=HIGH_PRECISION,
        preferred_element_type=jnp.float32,
    )
    total, numer = lax.psum((total, numer), ("seq", "sub"))
    landmark_values = numer / total[:, :, None]
    mixing_matrix = solve_mixing(query_head_rows, key_head_rows, landmark_values, score_scaling)
    scores_one = (
        jnp.einsum(
            "fxp,oxp->fxo",
            queries.reshape(row_count, H, HD),
            key_head_rows,
            preferred_element_type=jnp.float32,
        )
        * score_scaling
    )
    weight_matrix = row_softmax(scores_one).astype(jnp.bfloat16)
    attended = jnp.einsum(
        "ugf,gfa->uga", weight_matrix, mixing_matrix, preferred_element_type=jnp.float32
    )
    return attended.reshape(row_count, width).astype(jnp.bfloat16)


F32 = jnp.float32
BF16 = jnp.bfloat16
TN = (((0,), (0,)), ((), ()))
NN = (((1,), (0,)), ((), ()))
NT = (((1,), (1,)), ((), ()))


def dot(a, b, dims=NN):
    return lax.dot_general(a, b, dims, preferred_element_type=F32)


def split(a):
    high = a.astype(BF16)
    return high, (a - high.astype(F32)).astype(BF16)


def dot3(a, b, dims=NN):
    a_high, a_low = split(a)
    b_high, b_low = split(b)
    return dot(a_high, b_high, dims) + (dot(a_high, b_low, dims) + dot(a_low, b_high, dims))


def fused(
    n_seq,
    n_sub,
    q_ref,
    k_ref,
    v_ref,
    len_ref,
    out_ref,
    part,
    part_in,
    land,
    numer,
    numer_in,
    stats,
    stats_in,
    mix,
    weights,
    send_sem,
    recv_sem,
):
    n = n_seq * n_sub
    rows, width = q_ref.shape
    block = width // n
    per = HD // block
    pairs = H // 2
    scaling = 1.0 / math.sqrt(HD)
    me = lax.axis_index("seq") * n_sub + lax.axis_index("sub")

    def place(p):
        return {"seq": lax.div(p, n_sub), "sub": lax.rem(p, n_sub)}

    def peer(step):
        return lax.rem(me + step, n)

    def remote(phase, p, source, target):
        return pltpu.make_async_remote_copy(
            src_ref=source,
            dst_ref=target,
            send_sem=send_sem.at[phase, p],
            recv_sem=recv_sem.at[phase, me],
            device_id=place(p),
            device_id_type=pl.DeviceIdType.MESH,
        )

    def arrival(phase, p, target):
        pltpu.make_async_remote_copy(
            src_ref=target,
            dst_ref=target,
            send_sem=send_sem.at[phase, p],
            recv_sem=recv_sem.at[phase, p],
            device_id=place(p),
            device_id_type=pl.DeviceIdType.MESH,
        ).wait_recv()

    def each_peer(act):
        def body(step, carry):
            act(peer(step))
            return carry

        lax.fori_loop(1, n, body, 0)

    barrier = pltpu.get_barrier_semaphore()
    each_peer(
        lambda p: pl.semaphore_signal(
            barrier, inc=1, device_id=place(p), device_id_type=pl.DeviceIdType.MESH
        )
    )

    lengths = len_ref[...].astype(F32)
    upto = (
        lax.broadcasted_iota(jnp.int32, (M, M), 0) <= lax.broadcasted_iota(jnp.int32, (M, M), 1)
    ).astype(F32)
    ends = lax.dot_general(
        jnp.broadcast_to(lengths, (8, M)),
        upto,
        NN,
        precision=HIGH_PRECISION,
        preferred_element_type=F32,
    )[0:1]
    begins = ends - lengths
    positions = (me * rows + lax.broadcasted_iota(jnp.int32, (rows, M), 0)).astype(F32)
    member = ((positions >= begins) & (positions < ends)).astype(F32).astype(BF16)
    inverse_lengths = 1.0 / lengths
    for which, ref in enumerate((q_ref, k_ref)):
        means = (dot(ref[...], member, TN) * inverse_lengths).astype(BF16)
        for p in range(n):
            part[p, which * block : (which + 1) * block, :] = means[p * block : (p + 1) * block]

    pl.semaphore_wait(barrier, n - 1)
    each_peer(lambda p: remote(0, p, part.at[p], part_in.at[me]).start())

    def add_part(step, total):
        p = peer(step)
        arrival(0, p, part_in.at[p])
        return total + part_in[p].astype(F32)

    total = lax.fori_loop(1, n, add_part, part[me].astype(F32))
    land[me] = total.astype(BF16)
    each_peer(lambda p: remote(1, p, land.at[me], land.at[me]).start())

    first = lax.div(me, per) * per
    for i in range(per):
        p = first + i

        @pl.when(p != me)
        def _():
            arrival(1, p, land.at[p])

    q_head = jnp.concatenate([land[first + i, :block] for i in range(per)], axis=0)
    k_head = jnp.concatenate([land[first + i, block:] for i in range(per)], axis=0)
    scores = dot(q_head, k_head, TN) * scaling
    exponentials = jnp.exp(scores - jnp.max(scores, axis=1, keepdims=True))
    kernel_two = exponentials / jnp.sum(exponentials, axis=1, keepdims=True)
    absval = jnp.abs(kernel_two)
    row_most = jnp.max(jnp.sum(absval, axis=1, keepdims=True), axis=0, keepdims=True)
    col_most = jnp.max(jnp.sum(absval, axis=0, keepdims=True), axis=1, keepdims=True)
    inverse = kernel_two.T / (row_most * col_most)
    identity = (
        lax.broadcasted_iota(jnp.int32, (M, M), 0) == lax.broadcasted_iota(jnp.int32, (M, M), 1)
    ).astype(F32)
    for sweep in range(ITERS):
        product = dot3(kernel_two, inverse)
        nested = dot3(product, 7.0 * identity - product)
        nested = dot3(product, 15.0 * identity - nested)
        inverse = 0.25 * dot3(inverse, 13.0 * identity - nested)

    def other_arrival(p):
        @pl.when(lax.div(p, per) != lax.div(me, per))
        def _():
            arrival(1, p, land.at[p])

    each_peer(other_arrival)

    row = lax.broadcasted_iota(jnp.int32, (2 * HD, M), 0)

    def pair_operand(g, offset):
        both = jnp.concatenate(
            [land[p, offset : offset + block] for p in range(2 * g * per, 2 * (g + 1) * per)],
            axis=0,
        )
        zero = jnp.zeros_like(both)
        return jnp.concatenate(
            [jnp.where(row < HD, both, zero), jnp.where(row < HD, zero, both)], axis=1
        )

    stats[...] = jnp.zeros_like(stats)
    for g in range(pairs):
        lanes = slice(g * 2 * HD, (g + 1) * 2 * HD)
        scores = dot(k_ref[:, lanes], pair_operand(g, 0)) * scaling
        top = jnp.max(scores, axis=0, keepdims=True)
        exponentials = jnp.exp(scores - top)
        sums = jnp.sum(exponentials, axis=0, keepdims=True)
        both = dot(v_ref[:, lanes], exponentials.astype(BF16), TN)
        for side in range(2):
            head = 2 * g + side
            columns = slice(side * M, (side + 1) * M)
            stats[head, 0:1, :] = top[:, columns]
            stats[head, 1:2, :] = sums[:, columns]
            for i in range(per):
                begin = side * HD + i * block
                numer[head * per + i] = both[begin : begin + block, columns].astype(BF16)

    def send_numer(p):
        remote(2, p, numer.at[p], numer_in.at[me]).start()
        remote(3, p, stats.at[lax.div(p, per)], stats_in.at[me]).start()

    each_peer(send_numer)
    numer_in[me] = numer[me]
    stats_in[me] = stats[lax.div(me, per)]

    for g in range(pairs):
        lanes = slice(g * 2 * HD, (g + 1) * 2 * HD)
        scores = dot(q_ref[:, lanes], pair_operand(g, block)) * scaling
        for side in range(2):
            mine = scores[:, side * M : (side + 1) * M]
            weights[2 * g + side] = jnp.exp(mine - jnp.max(mine, axis=1, keepdims=True)).astype(BF16)

    def numer_arrival(p):
        arrival(2, p, numer_in.at[p])
        arrival(3, p, stats_in.at[p])

    each_peer(numer_arrival)
    tops = [stats_in[p, 0:1, :] for p in range(n)]
    top = functools.reduce(jnp.maximum, tops)
    total = jnp.zeros((1, M), F32)
    land_values = jnp.zeros((block, M), F32)
    for p in range(n):
        factor = jnp.exp(tops[p] - top)
        total += factor * stats_in[p, 1:2, :]
        land_values += factor * numer_in[p].astype(F32)
    mix[me] = dot3(land_values / total, inverse, NT).astype(BF16)
    each_peer(lambda p: remote(4, p, mix.at[me], mix.at[me]).start())
    each_peer(lambda p: arrival(4, p, mix.at[p]))

    ones = jnp.ones((HD, M), BF16)
    low = lax.broadcasted_iota(jnp.int32, (rows, 2 * HD), 1) < HD
    for g in range(pairs):
        mixed = [
            jnp.concatenate([mix[(2 * g + side) * per + i] for i in range(per)], axis=0)
            for side in range(2)
        ]
        left = dot(weights[2 * g], jnp.concatenate([mixed[0], ones], axis=0), NT)
        right = dot(weights[2 * g + 1], jnp.concatenate([ones, mixed[1]], axis=0), NT)
        sums = pltpu.roll(jnp.where(low, right, left), HD, 1)
        out_ref[:, g * 2 * HD : (g + 1) * 2 * HD] = (jnp.where(low, left, right) / sums).astype(BF16)

    def drain(p):
        remote(0, p, part.at[p], part_in.at[me]).wait_send()
        remote(1, p, land.at[me], land.at[me]).wait_send()
        remote(2, p, numer.at[p], numer_in.at[me]).wait_send()
        remote(3, p, stats.at[lax.div(p, per)], stats_in.at[me]).wait_send()
        remote(4, p, mix.at[me], mix.at[me]).wait_send()

    each_peer(drain)


def fused_shards(n_seq, n_sub, queries, keys, values, seg_lengths):
    n = n_seq * n_sub
    rows, width = queries.shape
    block = width // n
    vmem = pl.BlockSpec(memory_space=pltpu.VMEM)
    return pl.pallas_call(
        functools.partial(fused, n_seq, n_sub),
        out_shape=jax.ShapeDtypeStruct((rows, width), BF16),
        in_specs=[vmem] * 4,
        out_specs=vmem,
        scratch_shapes=[
            pltpu.VMEM((n, 2 * block, M), BF16),
            pltpu.VMEM((n, 2 * block, M), BF16),
            pltpu.VMEM((n, 2 * block, M), BF16),
            pltpu.VMEM((n, block, M), BF16),
            pltpu.VMEM((n, block, M), BF16),
            pltpu.VMEM((H, 8, M), F32),
            pltpu.VMEM((n, 8, M), F32),
            pltpu.VMEM((n, block, M), BF16),
            pltpu.VMEM((H, rows, M), BF16),
            pltpu.SemaphoreType.DMA((5, n)),
            pltpu.SemaphoreType.DMA((5, n)),
        ],
        compiler_params=pltpu.CompilerParams(
            collective_id=0, has_side_effects=True, vmem_limit_bytes=48 * 2**20
        ),
    )(queries, keys, values, seg_lengths.reshape(1, M))


def solution(mesh):
    placed = (
        P(("doc", "seq", "sub"), None),
        P(("doc", "seq", "sub"), None),
        P(("doc", "seq", "sub"), None),
        P("doc"),
    )
    n_seq, n_sub = mesh.shape["seq"], mesh.shape["sub"]
    block = H * HD // (n_seq * n_sub)
    whole_tiles = block % 16 == 0 and HD % block == 0 and block * n_seq * n_sub == H * HD
    return jax.shard_map(
        functools.partial(fused_shards, n_seq, n_sub) if whole_tiles else shards,
        mesh=mesh,
        in_specs=placed,
        out_specs=P(("doc", "seq", "sub"), None),
        check_vma=False,
    )
```

```python
import functools
import math

import jax
import jax.numpy as jnp
from jax import lax
from jax.experimental import pallas as pl
from jax.experimental.pallas import tpu as pltpu
from jax.sharding import PartitionSpec as P

H = 8
HD = 64
M = 256
ITERS = 3


HIGH_PRECISION = lax.Precision.HIGHEST


def row_softmax(score_matrix):
    row_top = lax.optimization_barrier(jnp.max(score_matrix, axis=-1, keepdims=True))
    exponentials = jnp.exp(score_matrix - row_top)
    return exponentials / lax.optimization_barrier(jnp.sum(exponentials, axis=-1, keepdims=True))


def iterative_pseudo_inverse(kernel):
    absval = jnp.abs(kernel)
    row_most = jnp.max(jnp.sum(absval, axis=2), axis=1)
    col_most = jnp.max(jnp.sum(absval, axis=1), axis=1)
    iterate = jnp.transpose(kernel, (0, 2, 1)) / (row_most * col_most)[:, None, None]
    identity = jnp.eye(kernel.shape[1], dtype=jnp.float32)[None]
    for sweep in range(ITERS):
        product = jnp.einsum("hij,hjk->hik", kernel, iterate, precision=HIGH_PRECISION)
        nested = jnp.einsum(
            "hij,hjk->hik", product, 7.0 * identity - product, precision=HIGH_PRECISION
        )
        nested = jnp.einsum(
            "hij,hjk->hik", product, 15.0 * identity - nested, precision=HIGH_PRECISION
        )
        iterate = 0.25 * jnp.einsum(
            "hij,hjk->hik", iterate, 13.0 * identity - nested, precision=HIGH_PRECISION
        )
    return iterate


def solve_mixing(query_head_rows, key_head_rows, landmark_values, score_scaling):
    landmark_kernel = row_softmax(
        jnp.einsum(
            "raj,taj->art", query_head_rows, key_head_rows, preferred_element_type=jnp.float32
        )
        * score_scaling
    )
    approx_inverse = iterative_pseudo_inverse(landmark_kernel)
    return jnp.einsum(
        "gux,gxr->gur", approx_inverse, landmark_values, precision=HIGH_PRECISION
    ).astype(jnp.bfloat16)


def shards(queries, keys, values, seg_lengths):
    row_count = queries.shape[0]
    width = queries.shape[1]
    score_scaling = 1.0 / math.sqrt(HD)
    shard = lax.axis_index("seq") * lax.axis_size("sub") + lax.axis_index("sub")
    positions = shard * row_count + lax.iota(jnp.int32, row_count)
    earlier = lax.broadcasted_iota(jnp.int32, (M, M), 0) <= lax.broadcasted_iota(jnp.int32, (M, M), 1)
    seg_ends = jnp.sum(jnp.where(earlier, seg_lengths[:, None], 0), axis=0)
    seg_begins = seg_ends - seg_lengths
    member = (
        (positions[:, None] >= seg_begins[None, :]) & (positions[:, None] < seg_ends[None, :])
    ).astype(jnp.bfloat16)
    counts = seg_lengths.astype(jnp.float32)
    contract = (((0,), (0,)), ((), ()))
    q_part = lax.dot_general(member, queries, contract, preferred_element_type=jnp.float32)
    k_part = lax.dot_general(member, keys, contract, preferred_element_type=jnp.float32)
    q_sums, k_sums = lax.psum((q_part, k_part), ("seq", "sub"))
    query_landmarks = (q_sums / counts[:, None]).astype(jnp.bfloat16)
    key_landmarks = (k_sums / counts[:, None]).astype(jnp.bfloat16)
    query_head_rows = query_landmarks.reshape(M, H, HD)
    key_head_rows = key_landmarks.reshape(M, H, HD)
    value_head_rows = values.reshape(row_count, H, HD)
    score_matrix = (
        jnp.einsum(
            "czy,rzy->zcr",
            query_head_rows,
            keys.reshape(row_count, H, HD),
            preferred_element_type=jnp.float32,
        )
        * score_scaling
    )
    row_top = lax.pmax(jnp.max(score_matrix, axis=2), ("seq", "sub"))
    exponentials = jnp.exp(score_matrix - row_top[:, :, None])
    total = jnp.sum(exponentials, axis=2)
    numer = jnp.einsum(
        "ijv,vib->ijb",
        exponentials,
        value_head_rows,
        precision=HIGH_PRECISION,
        preferred_element_type=jnp.float32,
    )
    total, numer = lax.psum((total, numer), ("seq", "sub"))
    landmark_values = numer / total[:, :, None]
    mixing_matrix = solve_mixing(query_head_rows, key_head_rows, landmark_values, score_scaling)
    scores_one = (
        jnp.einsum(
            "fxp,oxp->fxo",
            queries.reshape(row_count, H, HD),
            key_head_rows,
            preferred_element_type=jnp.float32,
        )
        * score_scaling
    )
    weight_matrix = row_softmax(scores_one).astype(jnp.bfloat16)
    attended = jnp.einsum(
        "ugf,gfa->uga", weight_matrix, mixing_matrix, preferred_element_type=jnp.float32
    )
    return attended.reshape(row_count, width).astype(jnp.bfloat16)


F32 = jnp.float32
BF16 = jnp.bfloat16
TN = (((0,), (0,)), ((), ()))
NN = (((1,), (0,)), ((), ()))
NT = (((1,), (1,)), ((), ()))


def dot(a, b, dims=NN):
    return lax.dot_general(a, b, dims, preferred_element_type=F32)


def split(a):
    high = a.astype(BF16)
    return high, (a - high.astype(F32)).astype(BF16)


def dot3(a, b, dims=NN):
    a_high, a_low = split(a)
    b_high, b_low = split(b)
    return dot(a_high, b_high, dims) + (dot(a_high, b_low, dims) + dot(a_low, b_high, dims))


def dot1(a, b, dims=NN):
    return dot(a.astype(BF16), b.astype(BF16), dims)


def fused(
    n_sub,
    q_hbm,
    k_hbm,
    v_hbm,
    len_ref,
    out_ref,
    q_ref,
    k_ref,
    v_ref,
    part,
    part_sib,
    part_out,
    part_in,
    land,
    numer,
    numer_sib,
    numer_out,
    numer_in,
    stats,
    stats_sib,
    stats_out,
    stats_in,
    mix,
    weights,
    load_sem,
    send_sem,
    recv_sem,
):
    rows = q_ref.shape[0]
    half = HD // 2
    pairs = H // 2
    scaling = 1.0 / math.sqrt(HD)
    me = lax.axis_index("seq") * n_sub + lax.axis_index("sub")
    core = lax.rem(me, 2)
    chip = lax.div(me, 2)
    other = 1 - core

    def place(p):
        return {"seq": lax.div(p, n_sub), "sub": lax.rem(p, n_sub)}

    def copy(phase, sent, landed, p, source, target):
        return pltpu.make_async_remote_copy(
            src_ref=source,
            dst_ref=target,
            send_sem=send_sem.at[phase, sent],
            recv_sem=recv_sem.at[phase, landed],
            device_id=place(p),
            device_id_type=pl.DeviceIdType.MESH,
        )

    def to_sibling(phase, slot, source, target):
        return copy(phase, slot, slot, 2 * chip + other, source, target)

    def to_chip(phase, c, source, target):
        return copy(phase, c, chip, 2 * c + core, source, target)

    def arrival(phase, slot, target):
        copy(phase, slot, slot, 2 * chip + other, target, target).wait_recv()

    def each_chip(act, first=1):
        def body(step, carry):
            act(lax.rem(chip + step, H))
            return carry

        lax.fori_loop(first, H, body, 0)

    loads = [
        pltpu.make_async_copy(source, target, load_sem.at[i])
        for i, (source, target) in enumerate(((q_hbm, q_ref), (k_hbm, k_ref), (v_hbm, v_ref)))
    ]
    for load in loads:
        load.start()
    barrier = pltpu.get_barrier_semaphore()

    def greet(p):
        pl.semaphore_signal(
            barrier, inc=1, device_id=place(p), device_id_type=pl.DeviceIdType.MESH
        )

    greet(2 * chip + other)
    each_chip(lambda c: greet(2 * c + core))

    lengths = len_ref[...].astype(F32)
    upto = (
        lax.broadcasted_iota(jnp.int32, (M, M), 0) <= lax.broadcasted_iota(jnp.int32, (M, M), 1)
    ).astype(F32)
    ends = lax.dot_general(
        jnp.broadcast_to(lengths, (8, M)),
        upto,
        NN,
        precision=HIGH_PRECISION,
        preferred_element_type=F32,
    )[0:1]
    begins = ends - lengths
    positions = (me * rows + lax.broadcasted_iota(jnp.int32, (rows, M), 0)).astype(F32)
    member = ((positions >= begins) & (positions < ends)).astype(F32).astype(BF16)
    inverse_lengths = 1.0 / lengths
    for which, ref in enumerate((q_ref, k_ref)):
        loads[which].wait()
        means = (dot(ref[...], member, TN) * inverse_lengths).astype(BF16)
        for c in range(H):
            part[which, c] = means[c * HD : (c + 1) * HD]

    pl.semaphore_wait(barrier, H)
    each_chip(lambda c: to_sibling(0, c, part.at[other, c], part_sib.at[c]).start())
    to_sibling(0, chip, part.at[other, chip], part_sib.at[chip]).start()

    def pass_part(c):
        arrival(0, c, part_sib.at[c])
        part_out[c] = (part[core, c].astype(F32) + part_sib[c].astype(F32)).astype(BF16)
        to_chip(1, c, part_out.at[c], part_in.at[chip]).start()

    each_chip(pass_part)
    arrival(0, chip, part_sib.at[chip])

    def add_part(step, total):
        c = lax.rem(chip + step, H)
        arrival(1, c, part_in.at[c])
        return total + part_in[c].astype(F32)

    total = part[core, chip].astype(F32) + part_sib[chip].astype(F32)
    land[core, chip] = lax.fori_loop(1, H, add_part, total).astype(BF16)
    to_sibling(3, chip, land.at[core, chip], land.at[core, chip]).start()
    each_chip(lambda c: to_chip(2, c, land.at[core, chip], land.at[core, chip]).start())

    arrival(3, chip, land.at[other, chip])
    scores = dot(land[0, chip], land[1, chip], TN) * scaling
    exponentials = jnp.exp(scores - jnp.max(scores, axis=1, keepdims=True))
    kernel_two = exponentials / jnp.sum(exponentials, axis=1, keepdims=True)
    absval = jnp.abs(kernel_two)
    row_most = jnp.max(jnp.sum(absval, axis=1, keepdims=True), axis=0, keepdims=True)
    col_most = jnp.max(jnp.sum(absval, axis=0, keepdims=True), axis=1, keepdims=True)
    inverse = kernel_two.T / (row_most * col_most)
    identity = (
        lax.broadcasted_iota(jnp.int32, (M, M), 0) == lax.broadcasted_iota(jnp.int32, (M, M), 1)
    ).astype(F32)

    def sweep(inverse, times):
        product = times(kernel_two, inverse)
        nested = times(product, 7.0 * identity - product)
        nested = times(product, 15.0 * identity - nested)
        return 0.25 * times(inverse, 13.0 * identity - nested)

    def pass_land(c):
        arrival(2, c, land.at[core, c])
        to_sibling(3, c, land.at[core, c], land.at[core, c]).start()

    each_chip(pass_land)
    each_chip(lambda c: arrival(3, c, land.at[other, c]))

    row = lax.broadcasted_iota(jnp.int32, (2 * HD, M), 0)

    def pair_operand(g, which):
        both = jnp.concatenate([land[which, 2 * g], land[which, 2 * g + 1]], axis=0)
        zero = jnp.zeros_like(both)
        return jnp.concatenate(
            [jnp.where(row < HD, both, zero), jnp.where(row < HD, zero, both)], axis=1
        )

    loads[2].wait()
    for g in range(pairs):
        lanes = slice(g * 2 * HD, (g + 1) * 2 * HD)
        scores = dot(k_ref[:, lanes], pair_operand(g, 0)) * scaling
        top = jnp.max(scores, axis=0, keepdims=True)
        exponentials = jnp.exp(scores - top)
        sums = jnp.sum(exponentials, axis=0, keepdims=True)
        both = dot(v_ref[:, lanes], exponentials.astype(BF16), TN)
        for side in range(2):
            head = 2 * g + side
            columns = slice(side * M, (side + 1) * M)
            stats[head] = pack_stats(top[:, columns], sums[:, columns])
            for c in range(2):
                begin = side * HD + c * half
                numer[c, head] = both[begin : begin + half, columns].astype(BF16)
            to_sibling(4, head, numer.at[other, head], numer_sib.at[head]).start()
            to_sibling(5, head, stats.at[head], stats_sib.at[head]).start()

    def merge(c):
        arrival(4, c, numer_sib.at[c])
        arrival(5, c, stats_sib.at[c])
        a_top, a_sum = unpack_stats(stats[c])
        b_top, b_sum = unpack_stats(stats_sib[c])
        top = jnp.maximum(a_top, b_top)
        a, b = jnp.exp(a_top - top), jnp.exp(b_top - top)
        values = a * numer[core, c].astype(F32) + b * numer_sib[c].astype(F32)
        return values.astype(BF16), pack_stats(top, a * a_sum + b * b_sum)

    def pass_numer(c):
        numer_out[c], stats_out[c] = merge(c)
        to_chip(6, c, numer_out.at[c], numer_in.at[chip]).start()
        to_chip(7, c, stats_out.at[c], stats_in.at[chip]).start()

    each_chip(pass_numer)
    numer_in[chip], stats_in[chip] = merge(chip)

    inverse = sweep(inverse, dot1)
    inverse = sweep(inverse, dot1)
    inverse = sweep(inverse, dot3)
    for g in range(pairs):
        lanes = slice(g * 2 * HD, (g + 1) * 2 * HD)
        scores = dot(q_ref[:, lanes], pair_operand(g, 1)) * scaling
        for side in range(2):
            mine = scores[:, side * M : (side + 1) * M]
            weights[2 * g + side] = jnp.exp(mine - jnp.max(mine, axis=1, keepdims=True)).astype(BF16)

    def numer_arrival(c):
        arrival(6, c, numer_in.at[c])
        arrival(7, c, stats_in.at[c])

    each_chip(numer_arrival)
    parts = [unpack_stats(stats_in[c]) for c in range(H)]
    top = functools.reduce(jnp.maximum, [part_top for part_top, _ in parts])
    total = jnp.zeros((1, M), F32)
    land_values = jnp.zeros((half, M), F32)
    for c, (part_top, part_sum) in enumerate(parts):
        factor = jnp.exp(part_top - top)
        total += factor * part_sum
        land_values += factor * numer_in[c].astype(F32)
    mix[core, chip] = dot3(land_values / total, inverse, NT).astype(BF16)
    each_chip(lambda c: to_chip(8, c, mix.at[core, chip], mix.at[core, chip]).start())
    to_sibling(9, chip, mix.at[core, chip], mix.at[core, chip]).start()

    def pass_mix(c):
        arrival(8, c, mix.at[core, c])
        to_sibling(9, c, mix.at[core, c], mix.at[core, c]).start()

    each_chip(pass_mix)
    each_chip(lambda c: arrival(9, c, mix.at[other, c]), 0)

    ones = jnp.ones((HD, M), BF16)
    low = lax.broadcasted_iota(jnp.int32, (rows, 2 * HD), 1) < HD
    for g in range(pairs):
        mixed = [
            jnp.concatenate([mix[c, 2 * g + side] for c in range(2)], axis=0) for side in range(2)
        ]
        left = dot(weights[2 * g], jnp.concatenate([mixed[0], ones], axis=0), NT)
        right = dot(weights[2 * g + 1], jnp.concatenate([ones, mixed[1]], axis=0), NT)
        sums = pltpu.roll(jnp.where(low, right, left), HD, 1)
        out_ref[:, g * 2 * HD : (g + 1) * 2 * HD] = (jnp.where(low, left, right) / sums).astype(BF16)

    def drain_chips(c):
        to_chip(1, c, part_out.at[c], part_in.at[chip]).wait_send()
        to_chip(2, c, land.at[core, chip], land.at[core, chip]).wait_send()
        to_chip(6, c, numer_out.at[c], numer_in.at[chip]).wait_send()
        to_chip(7, c, stats_out.at[c], stats_in.at[chip]).wait_send()
        to_chip(8, c, mix.at[core, chip], mix.at[core, chip]).wait_send()

    def drain_sibling(c):
        to_sibling(0, c, part.at[other, c], part_sib.at[c]).wait_send()
        to_sibling(3, c, land.at[core, c], land.at[core, c]).wait_send()
        to_sibling(4, c, numer.at[other, c], numer_sib.at[c]).wait_send()
        to_sibling(5, c, stats.at[c], stats_sib.at[c]).wait_send()
        to_sibling(9, c, mix.at[core, c], mix.at[core, c]).wait_send()

    each_chip(drain_chips)
    each_chip(drain_sibling, 0)


def pack_stats(top, total):
    halves = [x[:, i * M // 2 : (i + 1) * M // 2] for x in (top, total) for i in range(2)]
    return jnp.concatenate(halves + halves, axis=0)


def unpack_stats(tile):
    return (
        jnp.concatenate([tile[0:1], tile[1:2]], axis=1),
        jnp.concatenate([tile[2:3], tile[3:4]], axis=1),
    )


def fused_shards(n_sub, queries, keys, values, seg_lengths):
    rows, width = queries.shape
    vmem = pl.BlockSpec(memory_space=pltpu.VMEM)
    hbm = pl.BlockSpec(memory_space=pl.ANY)
    return pl.pallas_call(
        functools.partial(fused, n_sub),
        out_shape=jax.ShapeDtypeStruct((rows, width), BF16),
        in_specs=[hbm, hbm, hbm, vmem],
        out_specs=vmem,
        scratch_shapes=[pltpu.VMEM((rows, width), BF16)] * 3
        + [
            pltpu.VMEM((2, H, HD, M), BF16),
            pltpu.VMEM((H, HD, M), BF16),
            pltpu.VMEM((H, HD, M), BF16),
            pltpu.VMEM((H, HD, M), BF16),
            pltpu.VMEM((2, H, HD, M), BF16),
            pltpu.VMEM((2, H, HD // 2, M), BF16),
            pltpu.VMEM((H, HD // 2, M), BF16),
            pltpu.VMEM((H, HD // 2, M), BF16),
            pltpu.VMEM((H, HD // 2, M), BF16),
            pltpu.VMEM((H, 8, M // 2), F32),
            pltpu.VMEM((H, 8, M // 2), F32),
            pltpu.VMEM((H, 8, M // 2), F32),
            pltpu.VMEM((H, 8, M // 2), F32),
            pltpu.VMEM((2, H, HD // 2, M), BF16),
            pltpu.VMEM((H, rows, M), BF16),
            pltpu.SemaphoreType.DMA((3,)),
            pltpu.SemaphoreType.DMA((10, H)),
            pltpu.SemaphoreType.DMA((10, H)),
        ],
        compiler_params=pltpu.CompilerParams(
            collective_id=0, has_side_effects=True, vmem_limit_bytes=60 * 2**20
        ),
    )(queries, keys, values, seg_lengths.reshape(1, M))


def solution(mesh):
    placed = (
        P(("doc", "seq", "sub"), None),
        P(("doc", "seq", "sub"), None),
        P(("doc", "seq", "sub"), None),
        P("doc"),
    )
    n_seq, n_sub = mesh.shape["seq"], mesh.shape["sub"]
    chip_per_head = n_seq * n_sub == 2 * H and n_sub % 2 == 0
    return jax.shard_map(
        functools.partial(fused_shards, n_sub) if chip_per_head else shards,
        mesh=mesh,
        in_specs=placed,
        out_specs=P(("doc", "seq", "sub"), None),
        check_vma=False,
    )
```

```python
import functools
import math

import jax
import jax.numpy as jnp
from jax import lax
from jax.experimental import pallas as pl
from jax.experimental.pallas import tpu as pltpu
from jax.sharding import PartitionSpec as P

H = 8
HD = 64
M = 256
ITERS = 3


HIGH_PRECISION = lax.Precision.HIGHEST


def row_softmax(score_matrix):
    row_top = lax.optimization_barrier(jnp.max(score_matrix, axis=-1, keepdims=True))
    exponentials = jnp.exp(score_matrix - row_top)
    return exponentials / lax.optimization_barrier(jnp.sum(exponentials, axis=-1, keepdims=True))


def iterative_pseudo_inverse(kernel):
    absval = jnp.abs(kernel)
    row_most = jnp.max(jnp.sum(absval, axis=2), axis=1)
    col_most = jnp.max(jnp.sum(absval, axis=1), axis=1)
    iterate = jnp.transpose(kernel, (0, 2, 1)) / (row_most * col_most)[:, None, None]
    identity = jnp.eye(kernel.shape[1], dtype=jnp.float32)[None]
    for sweep in range(ITERS):
        product = jnp.einsum("hij,hjk->hik", kernel, iterate, precision=HIGH_PRECISION)
        nested = jnp.einsum(
            "hij,hjk->hik", product, 7.0 * identity - product, precision=HIGH_PRECISION
        )
        nested = jnp.einsum(
            "hij,hjk->hik", product, 15.0 * identity - nested, precision=HIGH_PRECISION
        )
        iterate = 0.25 * jnp.einsum(
            "hij,hjk->hik", iterate, 13.0 * identity - nested, precision=HIGH_PRECISION
        )
    return iterate


def solve_mixing(query_head_rows, key_head_rows, landmark_values, score_scaling):
    landmark_kernel = row_softmax(
        jnp.einsum(
            "raj,taj->art", query_head_rows, key_head_rows, preferred_element_type=jnp.float32
        )
        * score_scaling
    )
    approx_inverse = iterative_pseudo_inverse(landmark_kernel)
    return jnp.einsum(
        "gux,gxr->gur", approx_inverse, landmark_values, precision=HIGH_PRECISION
    ).astype(jnp.bfloat16)


def shards(queries, keys, values, seg_lengths):
    row_count = queries.shape[0]
    width = queries.shape[1]
    score_scaling = 1.0 / math.sqrt(HD)
    shard = lax.axis_index("seq") * lax.axis_size("sub") + lax.axis_index("sub")
    positions = shard * row_count + lax.iota(jnp.int32, row_count)
    earlier = lax.broadcasted_iota(jnp.int32, (M, M), 0) <= lax.broadcasted_iota(jnp.int32, (M, M), 1)
    seg_ends = jnp.sum(jnp.where(earlier, seg_lengths[:, None], 0), axis=0)
    seg_begins = seg_ends - seg_lengths
    member = (
        (positions[:, None] >= seg_begins[None, :]) & (positions[:, None] < seg_ends[None, :])
    ).astype(jnp.bfloat16)
    counts = seg_lengths.astype(jnp.float32)
    contract = (((0,), (0,)), ((), ()))
    q_part = lax.dot_general(member, queries, contract, preferred_element_type=jnp.float32)
    k_part = lax.dot_general(member, keys, contract, preferred_element_type=jnp.float32)
    q_sums, k_sums = lax.psum((q_part, k_part), ("seq", "sub"))
    query_landmarks = (q_sums / counts[:, None]).astype(jnp.bfloat16)
    key_landmarks = (k_sums / counts[:, None]).astype(jnp.bfloat16)
    query_head_rows = query_landmarks.reshape(M, H, HD)
    key_head_rows = key_landmarks.reshape(M, H, HD)
    value_head_rows = values.reshape(row_count, H, HD)
    score_matrix = (
        jnp.einsum(
            "czy,rzy->zcr",
            query_head_rows,
            keys.reshape(row_count, H, HD),
            preferred_element_type=jnp.float32,
        )
        * score_scaling
    )
    row_top = lax.pmax(jnp.max(score_matrix, axis=2), ("seq", "sub"))
    exponentials = jnp.exp(score_matrix - row_top[:, :, None])
    total = jnp.sum(exponentials, axis=2)
    numer = jnp.einsum(
        "ijv,vib->ijb",
        exponentials,
        value_head_rows,
        precision=HIGH_PRECISION,
        preferred_element_type=jnp.float32,
    )
    total, numer = lax.psum((total, numer), ("seq", "sub"))
    landmark_values = numer / total[:, :, None]
    mixing_matrix = solve_mixing(query_head_rows, key_head_rows, landmark_values, score_scaling)
    scores_one = (
        jnp.einsum(
            "fxp,oxp->fxo",
            queries.reshape(row_count, H, HD),
            key_head_rows,
            preferred_element_type=jnp.float32,
        )
        * score_scaling
    )
    weight_matrix = row_softmax(scores_one).astype(jnp.bfloat16)
    attended = jnp.einsum(
        "ugf,gfa->uga", weight_matrix, mixing_matrix, preferred_element_type=jnp.float32
    )
    return attended.reshape(row_count, width).astype(jnp.bfloat16)


F32 = jnp.float32
BF16 = jnp.bfloat16
TN = (((0,), (0,)), ((), ()))
NN = (((1,), (0,)), ((), ()))
NT = (((1,), (1,)), ((), ()))


def dot(a, b, dims=NN):
    return lax.dot_general(a, b, dims, preferred_element_type=F32)


def split(a):
    high = a.astype(BF16)
    return high, (a - high.astype(F32)).astype(BF16)


def dot3(a, b, dims=NN):
    a_high, a_low = split(a)
    b_high, b_low = split(b)
    return dot(a_high, b_high, dims) + (dot(a_high, b_low, dims) + dot(a_low, b_high, dims))


def dot1(a, b, dims=NN):
    return dot(a.astype(BF16), b.astype(BF16), dims)


def fused(
    n_sub,
    q_hbm,
    k_hbm,
    v_hbm,
    len_ref,
    out_ref,
    q_ref,
    k_ref,
    v_ref,
    part,
    part_sib,
    part_out,
    part_in,
    land,
    numer,
    numer_sib,
    numer_out,
    numer_in,
    stats,
    stats_sib,
    stats_out,
    stats_in,
    mix,
    weights,
    load_sem,
    send_sem,
    recv_sem,
):
    rows = q_ref.shape[0]
    half = HD // 2
    pairs = H // 2
    scaling = 1.0 / math.sqrt(HD)
    me = lax.axis_index("seq") * n_sub + lax.axis_index("sub")
    core = lax.rem(me, 2)
    chip = lax.div(me, 2)
    other = 1 - core

    def place(p):
        return {"seq": lax.div(p, n_sub), "sub": lax.rem(p, n_sub)}

    def copy(phase, sent, landed, p, source, target):
        return pltpu.make_async_remote_copy(
            src_ref=source,
            dst_ref=target,
            send_sem=send_sem.at[phase, sent],
            recv_sem=recv_sem.at[phase, landed],
            device_id=place(p),
            device_id_type=pl.DeviceIdType.MESH,
        )

    def to_sibling(phase, slot, source, target):
        return copy(phase, slot, slot, 2 * chip + other, source, target)

    def to_chip(phase, c, source, target):
        return copy(phase, c, chip, 2 * c + core, source, target)

    def arrival(phase, slot, target):
        copy(phase, slot, slot, 2 * chip + other, target, target).wait_recv()

    def each_chip(act, first=1):
        def body(step, carry):
            act(lax.rem(chip + step, H))
            return carry

        lax.fori_loop(first, H, body, 0)

    loads = [
        pltpu.make_async_copy(source, target, load_sem.at[i])
        for i, (source, target) in enumerate(((q_hbm, q_ref), (k_hbm, k_ref), (v_hbm, v_ref)))
    ]
    for load in loads:
        load.start()
    barrier = pltpu.get_barrier_semaphore()

    def greet(p):
        pl.semaphore_signal(
            barrier, inc=1, device_id=place(p), device_id_type=pl.DeviceIdType.MESH
        )

    greet(2 * chip + other)
    each_chip(lambda c: greet(2 * c + core))

    lengths = len_ref[...].astype(F32)
    upto = (
        lax.broadcasted_iota(jnp.int32, (M, M), 0) <= lax.broadcasted_iota(jnp.int32, (M, M), 1)
    ).astype(F32)
    ends = lax.dot_general(
        jnp.broadcast_to(lengths, (8, M)),
        upto,
        NN,
        precision=HIGH_PRECISION,
        preferred_element_type=F32,
    )[0:1]
    begins = ends - lengths
    positions = (me * rows + lax.broadcasted_iota(jnp.int32, (rows, M), 0)).astype(F32)
    member = ((positions >= begins) & (positions < ends)).astype(F32).astype(BF16)
    inverse_lengths = 1.0 / lengths
    def means_of(which, ref):
        loads[which].wait()
        means = (dot(ref[...], member, TN) * inverse_lengths).astype(BF16)
        for c in range(H):
            for side in range(2):
                begin = c * HD + side * half
                part[which, side, c] = means[begin : begin + half]

    def send_parts(which):
        each_chip(
            lambda c: to_sibling(
                10 * which, c, part.at[which, other, c], part_sib.at[which, c]
            ).start()
        )
        to_sibling(
            10 * which, chip, part.at[which, other, chip], part_sib.at[which, chip]
        ).start()

    def pass_parts(which):
        def pass_part(c):
            arrival(10 * which, c, part_sib.at[which, c])
            both = part[which, core, c].astype(F32) + part_sib[which, c].astype(F32)
            part_out[which, c] = both.astype(BF16)
            to_chip(
                10 * which + 1, c, part_out.at[which, c], part_in.at[which, chip]
            ).start()

        each_chip(pass_part)
        arrival(10 * which, chip, part_sib.at[which, chip])

    def add_parts(which):
        def add_part(step, total):
            c = lax.rem(chip + step, H)
            arrival(10 * which + 1, c, part_in.at[which, c])
            return total + part_in[which, c].astype(F32)

        total = part[which, core, chip].astype(F32) + part_sib[which, chip].astype(F32)
        land[which, core, chip] = lax.fori_loop(1, H, add_part, total).astype(BF16)
        mine = land.at[which, core, chip]
        each_chip(lambda c: to_chip(10 * which + 2, c, mine, mine).start())
        to_sibling(10 * which + 3, chip, mine, mine).start()

    def pass_lands(which):
        def pass_land(c):
            arrival(10 * which + 2, c, land.at[which, core, c])
            to_sibling(
                10 * which + 3, c, land.at[which, core, c], land.at[which, core, c]
            ).start()

        each_chip(pass_land)

    def await_lands(which):
        each_chip(lambda c: arrival(10 * which + 3, c, land.at[which, other, c]))

    means_of(0, q_ref)
    pl.semaphore_wait(barrier, H)
    send_parts(0)
    means_of(1, k_ref)
    pass_parts(0)
    send_parts(1)
    add_parts(0)
    pass_parts(1)
    pass_lands(0)
    arrival(3, chip, land.at[0, other, chip])
    await_lands(0)

    def head_land(which, c):
        return jnp.concatenate([land[which, side, c] for side in range(2)], axis=0)

    row = lax.broadcasted_iota(jnp.int32, (2 * HD, M), 0)

    def pair_operand(g, which):
        both = jnp.concatenate([head_land(which, 2 * g), head_land(which, 2 * g + 1)], axis=0)
        zero = jnp.zeros_like(both)
        return jnp.concatenate(
            [jnp.where(row < HD, both, zero), jnp.where(row < HD, zero, both)], axis=1
        )

    loads[2].wait()
    for g in range(pairs):
        lanes = slice(g * 2 * HD, (g + 1) * 2 * HD)
        scores = dot(k_ref[:, lanes], pair_operand(g, 0)) * scaling
        top = jnp.max(scores, axis=0, keepdims=True)
        exponentials = jnp.exp(scores - top)
        sums = jnp.sum(exponentials, axis=0, keepdims=True)
        both = dot(v_ref[:, lanes], exponentials.astype(BF16), TN)
        for side in range(2):
            head = 2 * g + side
            columns = slice(side * M, (side + 1) * M)
            stats[head] = pack_stats(top[:, columns], sums[:, columns])
            for c in range(2):
                begin = side * HD + c * half
                numer[c, head] = both[begin : begin + half, columns].astype(BF16)
            to_sibling(4, head, numer.at[other, head], numer_sib.at[head]).start()
            to_sibling(5, head, stats.at[head], stats_sib.at[head]).start()

    def merge(c):
        arrival(4, c, numer_sib.at[c])
        arrival(5, c, stats_sib.at[c])
        a_top, a_sum = unpack_stats(stats[c])
        b_top, b_sum = unpack_stats(stats_sib[c])
        top = jnp.maximum(a_top, b_top)
        a, b = jnp.exp(a_top - top), jnp.exp(b_top - top)
        values = a * numer[core, c].astype(F32) + b * numer_sib[c].astype(F32)
        return values.astype(BF16), pack_stats(top, a * a_sum + b * b_sum)

    def pass_numer(c):
        numer_out[c], stats_out[c] = merge(c)
        to_chip(6, c, numer_out.at[c], numer_in.at[chip]).start()
        to_chip(7, c, stats_out.at[c], stats_in.at[chip]).start()

    each_chip(pass_numer)
    numer_in[chip], stats_in[chip] = merge(chip)

    add_parts(1)
    arrival(13, chip, land.at[1, other, chip])
    scores = dot(head_land(0, chip), head_land(1, chip), TN) * scaling
    exponentials = jnp.exp(scores - jnp.max(scores, axis=1, keepdims=True))
    kernel_two = exponentials / jnp.sum(exponentials, axis=1, keepdims=True)
    absval = jnp.abs(kernel_two)
    row_most = jnp.max(jnp.sum(absval, axis=1, keepdims=True), axis=0, keepdims=True)
    col_most = jnp.max(jnp.sum(absval, axis=0, keepdims=True), axis=1, keepdims=True)
    inverse = kernel_two.T / (row_most * col_most)
    identity = (
        lax.broadcasted_iota(jnp.int32, (M, M), 0) == lax.broadcasted_iota(jnp.int32, (M, M), 1)
    ).astype(F32)

    def sweep(inverse, times):
        product = times(kernel_two, inverse)
        nested = times(product, 7.0 * identity - product)
        nested = times(product, 15.0 * identity - nested)
        return 0.25 * times(inverse, 13.0 * identity - nested)

    inverse = sweep(inverse, dot1)
    inverse = sweep(inverse, dot1)
    inverse = sweep(inverse, dot3)
    pass_lands(1)

    def numer_arrival(c):
        arrival(6, c, numer_in.at[c])
        arrival(7, c, stats_in.at[c])

    each_chip(numer_arrival)
    parts = [unpack_stats(stats_in[c]) for c in range(H)]
    top = functools.reduce(jnp.maximum, [part_top for part_top, _ in parts])
    total = jnp.zeros((1, M), F32)
    land_values = jnp.zeros((half, M), F32)
    for c, (part_top, part_sum) in enumerate(parts):
        factor = jnp.exp(part_top - top)
        total += factor * part_sum
        land_values += factor * numer_in[c].astype(F32)
    mix[core, chip] = dot3(land_values / total, inverse, NT).astype(BF16)
    each_chip(lambda c: to_chip(8, c, mix.at[core, chip], mix.at[core, chip]).start())
    to_sibling(9, chip, mix.at[core, chip], mix.at[core, chip]).start()

    await_lands(1)
    for g in range(pairs):
        lanes = slice(g * 2 * HD, (g + 1) * 2 * HD)
        scores = dot(q_ref[:, lanes], pair_operand(g, 1)) * scaling
        for side in range(2):
            mine = scores[:, side * M : (side + 1) * M]
            weights[2 * g + side] = jnp.exp(mine - jnp.max(mine, axis=1, keepdims=True)).astype(BF16)

    def pass_mix(c):
        arrival(8, c, mix.at[core, c])
        to_sibling(9, c, mix.at[core, c], mix.at[core, c]).start()

    each_chip(pass_mix)
    each_chip(lambda c: arrival(9, c, mix.at[other, c]), 0)

    ones = jnp.ones((HD, M), BF16)
    low = lax.broadcasted_iota(jnp.int32, (rows, 2 * HD), 1) < HD
    for g in range(pairs):
        mixed = [
            jnp.concatenate([mix[c, 2 * g + side] for c in range(2)], axis=0) for side in range(2)
        ]
        left = dot(weights[2 * g], jnp.concatenate([mixed[0], ones], axis=0), NT)
        right = dot(weights[2 * g + 1], jnp.concatenate([ones, mixed[1]], axis=0), NT)
        sums = pltpu.roll(jnp.where(low, right, left), HD, 1)
        out_ref[:, g * 2 * HD : (g + 1) * 2 * HD] = (jnp.where(low, left, right) / sums).astype(BF16)

    def drain_chips(c):
        for which in range(2):
            mine = land.at[which, core, chip]
            to_chip(
                10 * which + 1, c, part_out.at[which, c], part_in.at[which, chip]
            ).wait_send()
            to_chip(10 * which + 2, c, mine, mine).wait_send()
        to_chip(6, c, numer_out.at[c], numer_in.at[chip]).wait_send()
        to_chip(7, c, stats_out.at[c], stats_in.at[chip]).wait_send()
        to_chip(8, c, mix.at[core, chip], mix.at[core, chip]).wait_send()

    def drain_sibling(c):
        for which in range(2):
            block = land.at[which, core, c]
            to_sibling(
                10 * which, c, part.at[which, other, c], part_sib.at[which, c]
            ).wait_send()
            to_sibling(10 * which + 3, c, block, block).wait_send()
        to_sibling(4, c, numer.at[other, c], numer_sib.at[c]).wait_send()
        to_sibling(5, c, stats.at[c], stats_sib.at[c]).wait_send()
        to_sibling(9, c, mix.at[core, c], mix.at[core, c]).wait_send()

    each_chip(drain_chips)
    each_chip(drain_sibling, 0)


def pack_stats(top, total):
    halves = [x[:, i * M // 2 : (i + 1) * M // 2] for x in (top, total) for i in range(2)]
    return jnp.concatenate(halves + halves, axis=0)


def unpack_stats(tile):
    return (
        jnp.concatenate([tile[0:1], tile[1:2]], axis=1),
        jnp.concatenate([tile[2:3], tile[3:4]], axis=1),
    )


def fused_shards(n_sub, queries, keys, values, seg_lengths):
    rows, width = queries.shape
    vmem = pl.BlockSpec(memory_space=pltpu.VMEM)
    hbm = pl.BlockSpec(memory_space=pl.ANY)
    return pl.pallas_call(
        functools.partial(fused, n_sub),
        out_shape=jax.ShapeDtypeStruct((rows, width), BF16),
        in_specs=[hbm, hbm, hbm, vmem],
        out_specs=vmem,
        scratch_shapes=[pltpu.VMEM((rows, width), BF16)] * 3
        + [
            pltpu.VMEM((2, 2, H, HD // 2, M), BF16),
            pltpu.VMEM((2, H, HD // 2, M), BF16),
            pltpu.VMEM((2, H, HD // 2, M), BF16),
            pltpu.VMEM((2, H, HD // 2, M), BF16),
            pltpu.VMEM((2, 2, H, HD // 2, M), BF16),
            pltpu.VMEM((2, H, HD // 2, M), BF16),
            pltpu.VMEM((H, HD // 2, M), BF16),
            pltpu.VMEM((H, HD // 2, M), BF16),
            pltpu.VMEM((H, HD // 2, M), BF16),
            pltpu.VMEM((H, 8, M // 2), F32),
            pltpu.VMEM((H, 8, M // 2), F32),
            pltpu.VMEM((H, 8, M // 2), F32),
            pltpu.VMEM((H, 8, M // 2), F32),
            pltpu.VMEM((2, H, HD // 2, M), BF16),
            pltpu.VMEM((H, rows, M), BF16),
            pltpu.SemaphoreType.DMA((3,)),
            pltpu.SemaphoreType.DMA((14, H)),
            pltpu.SemaphoreType.DMA((14, H)),
        ],
        compiler_params=pltpu.CompilerParams(
            collective_id=0, has_side_effects=True, vmem_limit_bytes=60 * 2**20
        ),
    )(queries, keys, values, seg_lengths.reshape(1, M))


def solution(mesh):
    placed = (
        P(("doc", "seq", "sub"), None),
        P(("doc", "seq", "sub"), None),
        P(("doc", "seq", "sub"), None),
        P("doc"),
    )
    n_seq, n_sub = mesh.shape["seq"], mesh.shape["sub"]
    chip_per_head = n_seq * n_sub == 2 * H and n_sub % 2 == 0
    return jax.shard_map(
        functools.partial(fused_shards, n_sub) if chip_per_head else shards,
        mesh=mesh,
        in_specs=placed,
        out_specs=P(("doc", "seq", "sub"), None),
        check_vma=False,
    )
```
